32 devices in a mesh: line: 16 (over z, x, core), bus: 2 (over y).
Axes of the slice: x: 2, y: 2, z: 4, core: 2. Of those that a mesh axis runs over, the one named last changes fastest.
Arguments:
- injections: float32 [1024, 8192], P('line', 'bus'), may hold values from -6 to 6
- shift_factors: float32 [16384, 8192], P('line', 'bus'), may hold values from -0.0625 to 0.0625
- line_rating: int32 [1024, 16384], P(None, 'line'), may hold values from 40 to 159
- retention: float32 [1024, 256], P('line', 'bus'), may hold values from 0.5 to 1
- discharge: float32 [256], P('bus'), may hold values from 0.05 to 0.5
- profile: float32 [1024, 256], P('line', 'bus'), may hold values from -6 to 6
- storage_bus: int32 [256], P('bus'), may hold values from 0 to 8191, as said below
- online_hour: int32 [256], P('bus'), may hold values from 0 to 511
Outputs:
- bus_adjoint: float32 [1024, 8192], P('line', 'bus')
- size_grad: float32 [256], P('bus')
The draws below stay inside these ranges and needn't reach their ends.
Inputs may be any that keep to these rules, and one draw needn't show every extreme that they name: `storage_bus`: unit k sits at a bus of index from (k // 128) * 4096 to (k // 128 + 1) * 4096 - 1.
All inputs are finite; a program needn't handle non-finite values.
Results may differ from the reference program's by a relative error of at most 0.0003.
Values sent between devices are 32-bit elements; how exact they have to be, the bound alone decides.
A program may use at most 128 MiB of HBM per device.

```python
import math
import jax
import jax.numpy as jnp
from jax import lax

LINES = 16384
BUSES = 8192
STORE_DEV = 128
PERIOD_LENGTH = 1024
STORES = 256
BUS_DEV = 4096


def draw_retention(key, part):
    sampler_seeds = jax.random.split(jax.random.fold_in(key, 11), 6)
    slow = jax.random.uniform(sampler_seeds[0], (STORES,)) < 0.5
    kept_total = jax.random.uniform(sampler_seeds[1], (STORES,), minval=0.4, maxval=0.8)
    fast_rate = jax.random.uniform(sampler_seeds[2], (STORES,), minval=1.0 / 50.0, maxval=1.0 / 30.0)
    leakage_fraction = jnp.where(slow, -jnp.log(kept_total) / PERIOD_LENGTH, fast_rate)
    noisy_demand_series = jax.random.uniform(sampler_seeds[3], (PERIOD_LENGTH, STORES), minval=0.5, maxval=1.5)
    spike_withdrawal = jax.random.uniform(sampler_seeds[4], (PERIOD_LENGTH, 1)) < 3.0 / PERIOD_LENGTH
    congestion_penalty_value = jax.random.uniform(sampler_seeds[5], (PERIOD_LENGTH, STORES), minval=0.2, maxval=0.4)
    retained_charge = jnp.exp(-leakage_fraction[None, :] * noisy_demand_series) * jnp.where(spike_withdrawal, 1.0 - congestion_penalty_value, 1.0)
    return retained_charge.astype(jnp.float32)


def draw_storage_bus(key, part):
    position = jax.random.randint(jax.random.fold_in(key, 23), (STORES,), 0, BUS_DEV)
    position = position.at[0].set(0).at[STORES - 1].set(BUS_DEV - 1)
    owner = jnp.arange(STORES, dtype=jnp.int32) // STORE_DEV
    return (owner * BUS_DEV + position).astype(jnp.int32)


def touch_ends(entries, stream_key, least, high):
    longest = entries.shape.index(max(entries.shape))
    spots = []
    for shift in (0, 1):
        where = [jax.random.randint(jax.random.fold_in(stream_key, axis), (), 0, length) for axis, length in enumerate(entries.shape)]
        where[longest] = (where[longest] + shift) % entries.shape[longest]
        spots.append(tuple(where))
    return entries.at[spots[0]].set(least).at[spots[1]].set(high)


def steps_of(own_key, dims, cuts, smallest, high):
    loudness, own = 1.0, jax.random.fold_in(own_key, 6)
    for dim, parts in cuts:
        heights = jnp.exp(jax.random.uniform(jax.random.fold_in(own, dim), (parts,), jnp.float32, smallest / len(cuts), high / len(cuts)))
        loudness = loudness * jnp.repeat(heights, dims[dim] // parts).reshape([-1 if axis == dim else 1 for axis in range(len(dims))])
    return loudness


def gaussian(rng, extent, spread, limit, cuts=(), kind=jnp.bfloat16):
    drawn = jax.random.normal(rng, extent, jnp.float32) * spread
    if len(cuts) > 0:
        drawn = steps_of(rng, extent, cuts, -0.22, 0.18) * drawn
    return jnp.clip(drawn, min=-limit, max=limit).astype(kind)


def setup_inputs(seed: int = 0) -> dict:
    key_list = jax.random.split(jax.random.key(seed), 9)
    return {
        "injections": gaussian(key_list[0], (PERIOD_LENGTH, BUSES), 1.0, 6.0, ((0, 16), (1, 2)), jnp.float32),
        "shift_factors": gaussian(key_list[1], (LINES, BUSES), BUSES ** -0.5, 0.0625, ((0, 16), (1, 2)), jnp.float32),
        "line_rating": touch_ends(jax.random.randint(key_list[2], (PERIOD_LENGTH, LINES), 40, 160), jax.random.fold_in(key_list[2], 1), 40, 159).astype(jnp.int32),
        "retention": draw_retention(jax.random.fold_in(key_list[8], 71), 0),
        "discharge": jnp.clip(jnp.exp(math.log(0.5) - 2.3025851 * jax.random.uniform(key_list[4], (STORES,), jnp.float32) ** steps_of(key_list[4], (STORES,), ((0, 2),), -0.2, 0.2)), 0.05, 0.5),
        "profile": gaussian(key_list[5], (PERIOD_LENGTH, STORES), 1.0, 6.0, ((0, 16), (1, 2)), jnp.float32),
        "storage_bus": draw_storage_bus(jax.random.fold_in(key_list[8], 71), 0),
        "online_hour": touch_ends(jax.random.randint(key_list[7], (STORES,), 0, PERIOD_LENGTH // 2), jax.random.fold_in(key_list[7], 1), 0, (PERIOD_LENGTH // 2) - 1).astype(jnp.int32),
    }


def reference(injections, shift_factors, line_rating, retention, discharge, profile, storage_bus, online_hour):
    highest = lax.Precision.HIGHEST
    line_flows = jnp.dot(injections, shift_factors.T, precision=highest, preferred_element_type=jnp.float32)
    limits = line_rating.astype(jnp.float32) * 0.01
    excess = jnp.maximum(jnp.abs(line_flows) - limits, 0.0)
    flow_adjoint = excess * jnp.sign(line_flows)
    bus_adjoint = jnp.dot(flow_adjoint, shift_factors, precision=highest, preferred_element_type=jnp.float32)
    source = discharge[None, :] * bus_adjoint[:, storage_bus]

    def backward_step(carried, hour_inputs):
        source_now, keep_now = hour_inputs
        costate_now = source_now + carried
        return (keep_now * costate_now, costate_now)
    _, costate = lax.scan(backward_step, jnp.zeros((STORES,), jnp.float32), (source, retention), reverse=True)
    hour_index = jnp.arange(PERIOD_LENGTH, dtype=jnp.int32)
    active = (hour_index[:, None] >= online_hour[None, :]).astype(jnp.float32)
    size_grad = lax.optimization_barrier(jnp.sum(costate * profile * active, axis=0)) / math.sqrt(PERIOD_LENGTH)
    return (bus_adjoint, size_grad)
```

```python
import functools
import math

import jax
import jax.numpy as jnp
from jax import lax
from jax.experimental import pallas as pl
from jax.experimental.pallas import tpu as pltpu
from jax.sharding import PartitionSpec as P

MESH = pl.DeviceIdType.MESH
F32, BF16 = jnp.float32, jnp.bfloat16


def split(value):
    high = value.astype(BF16)
    return high, (value - high.astype(F32)).astype(BF16)


def dot3(a_hi, a_lo, b_hi, b_lo, dims):
    dot = functools.partial(
        lax.dot_general, dimension_numbers=(dims, ((), ())), preferred_element_type=F32
    )
    return dot(a_hi, b_hi) + (dot(a_hi, b_lo) + dot(a_lo, b_hi))


def tile_of(width, most):
    return math.gcd(width, most)


def kernel(
    planes, bus_count,
    inj, factors, rating, retention, discharge, profile, local_bus, online,
    out, stats, gathered,
    s_hi, s_lo, stage, x_hi, x_lo, flows, flows_in, a_hi, a_lo, limit, part,
    from_core, from_x, from_z, source,
    local_sem,
    gz_send, gz_recv, gx_send, gx_recv, gc_send, gc_recv,
    y_send, y_recv, rc_send, rc_recv, rx_send, rx_recv, rz_send, rz_recv,
):
    line, bus = lax.axis_index("line"), lax.axis_index("bus")
    z, x, c = line // 4, (line // 2) % 2, line % 2
    me = 2 * x + c
    hours, buses = inj.shape
    lines = factors.shape[0]
    chunk = 4 * hours

    def at(plane, column, core):
        return (plane * 4 + column * 2 + core, bus)

    sibling, across = at(z, x, 1 - c), at(z, 1 - x, c)

    def plane_of(s):
        both = jnp.minimum(z, planes - 1 - z)
        away = (s + 1) // 2
        near = jnp.where(s % 2 == 1, z - away, z + away)
        far = jnp.where(z < planes - 1 - z, s, planes - 1 - s)
        return jnp.where(s <= 2 * both, near, far)

    def rows(block):
        return pl.ds(pl.multiple_of(block * hours, hours), hours)

    def block_copy(plane, block, send, recv, target):
        ref = gathered.at[plane, rows(block)]
        return pltpu.make_async_remote_copy(
            src_ref=ref, dst_ref=ref, send_sem=send, recv_sem=recv,
            device_id=target, device_id_type=MESH,
        )

    def along_z(plane, way, target_plane):
        return block_copy(
            plane, me, gz_send.at[way, plane], gz_recv.at[plane], at(target_plane, x, c)
        )

    def to_across(plane):
        return block_copy(plane, me, gx_send.at[plane], gx_recv.at[plane], across)

    def from_across(plane):
        return block_copy(
            plane, 2 * (1 - x) + c, gx_send.at[plane], gx_recv.at[plane], across
        )

    def to_sibling(plane, k):
        block = 2 * (x if k == 0 else 1 - x) + c
        return block_copy(plane, block, gc_send.at[k, plane], gc_recv.at[k, plane], sibling)

    def from_sibling(plane, k):
        block = 2 * (x if k == 0 else 1 - x) + 1 - c
        return block_copy(plane, block, gc_send.at[k, plane], gc_recv.at[k, plane], sibling)

    def goes_up(plane):
        return (plane <= z) & (z + 1 < planes)

    def goes_down(plane):
        return (plane >= z) & (z > 0)

    def forward(s):
        plane = plane_of(s)

        @pl.when(s > 0)
        def _():
            along_z(plane, 0, z).wait_recv()

        @pl.when(goes_up(plane))
        def _():
            along_z(plane, 0, z + 1).start()

        @pl.when(goes_down(plane))
        def _():
            along_z(plane, 1, z - 1).start()

        to_across(plane).start()
        to_sibling(plane, 0).start()

    def forward_across(s):
        plane = plane_of(s)
        from_across(plane).wait_recv()
        to_sibling(plane, 1).start()

    def flow_copy(s, r):
        return pltpu.make_async_remote_copy(
            src_ref=flows.at[s], dst_ref=flows_in.at[s, r - 1],
            send_sem=y_send.at[s, r - 1], recv_sem=y_recv.at[s, r - 1],
            device_id=(line, (bus + r) % bus_count), device_id_type=MESH,
        )

    def first_product(s):
        plane = plane_of(s)
        from_sibling(plane, 0).wait_recv()
        from_sibling(plane, 1).wait_recv()
        load = pltpu.make_async_copy(gathered.at[plane], stage, local_sem.at[0])
        load.start()
        load.wait()
        step = tile_of(chunk, 32)

        @pl.loop(0, chunk // step)
        def _(i):
            here = pl.ds(pl.multiple_of(i * step, step), step)
            x_hi[here], x_lo[here] = split(stage[here])

        width = tile_of(lines, 256)

        @pl.loop(0, lines // width)
        def _(n):
            here = pl.ds(pl.multiple_of(n * width, width), width)
            flows[s, :, here] = dot3(
                x_hi[...], x_lo[...], s_hi[here], s_lo[here], ((1,), (1,))
            )

        for r in range(1, bus_count):
            flow_copy(s, r).start()

    def core_copy(s, k):
        return pltpu.make_async_remote_copy(
            src_ref=part.at[2 * k + 1 - c], dst_ref=from_core.at[s, k],
            send_sem=rc_send.at[s, k], recv_sem=rc_recv.at[s, k],
            device_id=sibling, device_id_type=MESH,
        )

    def x_copy(s):
        return pltpu.make_async_remote_copy(
            src_ref=from_core.at[s, 1 - x], dst_ref=from_x.at[s],
            send_sem=rx_send.at[s], recv_sem=rx_recv.at[s],
            device_id=across, device_id_type=MESH,
        )

    def z_copy(s):
        plane = plane_of(s)
        return pltpu.make_async_remote_copy(
            src_ref=from_x.at[s], dst_ref=from_z.at[z],
            send_sem=rz_send.at[s], recv_sem=rz_recv.at[z],
            device_id=at(plane, x, c), device_id_type=MESH,
        )

    def second_product(s):
        plane = plane_of(s)
        here = pl.ds(pl.multiple_of(plane * chunk, chunk), chunk)
        load = pltpu.make_async_copy(rating.at[here], limit, local_sem.at[0])
        load.start()
        for r in range(1, bus_count):
            flow_copy(s, r).wait_recv()
        load.wait()
        step = tile_of(chunk, 32)

        @pl.loop(0, chunk // step)
        def _(i):
            here = pl.ds(pl.multiple_of(i * step, step), step)
            total = flows[s, here]
            for r in range(1, bus_count):
                total = total + flows_in[s, r - 1, here]
            bound = limit[here].astype(F32) * 0.01
            adjoint = jnp.where(
                total > bound, total - bound, jnp.where(total < -bound, total + bound, 0.0)
            )
            a_hi[here], a_lo[here] = split(adjoint)

        width = tile_of(buses, 512)

        @pl.loop(0, buses // width)
        def _(n):
            here = pl.ds(pl.multiple_of(n * width, width), width)
            value = dot3(a_hi[...], a_lo[...], s_hi[:, here], s_lo[:, here], ((1,), (0,)))
            for block in range(4):
                part[block, :, here] = value[block * hours : (block + 1) * hours]

        for k in range(2):
            core_copy(s, k).start()

    def add_to(ref, *others):
        step = tile_of(hours, 8)

        @pl.loop(0, hours // step)
        def _(i):
            here = pl.ds(pl.multiple_of(i * step, step), step)
            total = ref[here]
            for other in others:
                total = total + other[here]
            ref[here] = total

    def reduce_across(s):
        for k in range(2):
            core_copy(s, k).wait_recv()
        add_to(from_core.at[s, 1 - x], part.at[2 * (1 - x) + c])
        x_copy(s).start()
        add_to(from_core.at[s, x], part.at[me])
        for k in range(2):
            core_copy(s, k).wait_send()

    def reduce_along(s):
        x_copy(s).wait_recv()
        add_to(from_x.at[s], from_core.at[s, x])

        @pl.when(s > 0)
        def _():
            z_copy(s).start()

    barrier = pltpu.get_barrier_semaphore()
    mine = pltpu.make_async_copy(inj, gathered.at[z, rows(me)], local_sem.at[0])
    mine.start()
    for target in (sibling, across):
        pl.semaphore_signal(barrier, inc=1, device_id=target, device_id_type=MESH)
    for r in range(1, planes):
        pl.semaphore_signal(
            barrier, inc=1, device_id=at((z + r) % planes, x, c), device_id_type=MESH
        )
    for r in range(1, bus_count):
        pl.semaphore_signal(
            barrier, inc=1, device_id=(line, (bus + r) % bus_count), device_id_type=MESH
        )
    mine.wait()
    pl.semaphore_wait(barrier, planes + bus_count)
    forward(0)

    group = tile_of(lines, chunk)

    def factor_load(i):
        here = pl.ds(pl.multiple_of(i * group, group), group)
        return pltpu.make_async_copy(factors.at[here], stage.at[pl.ds(0, group)], local_sem.at[0])

    @pl.loop(0, lines // group)
    def _(i):
        factor_load(i).start()
        factor_load(i).wait()
        step = tile_of(group, 16)

        @pl.loop(0, group // step)
        def _(j):
            here = pl.ds(pl.multiple_of(j * step, step), step)
            there = pl.ds(pl.multiple_of(i * group + j * step, step), step)
            s_hi[there], s_lo[there] = split(stage[here])

    @pl.loop(0, planes + 3)
    def _(t):
        @pl.when(t + 1 < planes)
        def _():
            forward(t + 1)

        @pl.when(t < planes)
        def _():
            forward_across(t)
            first_product(t)

        @pl.when((t >= 2) & (t < planes + 2))
        def _():
            s = (t - 1) % planes
            second_product(s)
            reduce_across(s)

        @pl.when(t >= 3)
        def _():
            reduce_along((t - 2) % planes)

    total = from_x.at[0]
    for r in range(1, planes):
        other = (z + r) % planes
        pltpu.make_async_remote_copy(
            src_ref=from_x.at[0], dst_ref=from_z.at[other],
            send_sem=rz_send.at[0], recv_sem=rz_recv.at[other],
            device_id=at(other, x, c), device_id_type=MESH,
        ).wait_recv()
        add_to(total, from_z.at[other])
    store = pltpu.make_async_copy(total, out, local_sem.at[0])
    store.start()

    width = tile_of(buses, 512)
    source[...] = jnp.zeros_like(source)

    @pl.loop(0, buses // width)
    def _(n):
        here = pl.ds(pl.multiple_of(n * width, width), width)
        place = n * width + lax.broadcasted_iota(jnp.int32, (width, source.shape[1]), 0)
        chosen = jnp.where(place == local_bus[...], 1.0, 0.0).astype(BF16)
        left = total[:, here]
        for _ in range(3):
            high = left.astype(BF16)
            left = left - high.astype(F32)
            source[...] += jnp.dot(high, chosen, preferred_element_type=F32)

    def hour_back(i, carried):
        carry, gain, fixed, slope = carried
        t = hours - 1 - i
        keep = retention[pl.ds(t, 1), :]
        weight = jnp.where(line * hours + t >= online[...], profile[pl.ds(t, 1), :], 0.0)
        costate = discharge[...] * source[pl.ds(t, 1), :] + carry
        return (keep * costate, keep * gain, fixed + costate * weight, slope + gain * weight)

    zero = jnp.zeros((1, source.shape[1]), F32)
    done = lax.fori_loop(0, hours, hour_back, (zero, zero + 1.0, zero, zero))
    stats[...] = jnp.zeros_like(stats)
    for i in range(4):
        stats[i : i + 1, :] = done[i]

    store.wait()

    @pl.loop(0, planes)
    def _(s):
        plane = plane_of(s)

        @pl.when(goes_up(plane))
        def _():
            along_z(plane, 0, z + 1).wait_send()

        @pl.when(goes_down(plane))
        def _():
            along_z(plane, 1, z - 1).wait_send()

        to_across(plane).wait_send()
        for k in range(2):
            to_sibling(plane, k).wait_send()
        for r in range(1, bus_count):
            flow_copy(s, r).wait_send()
        x_copy(s).wait_send()

        @pl.when(s > 0)
        def _():
            z_copy(s).wait_send()


def on_device(
    planes, bus_count,
    injections, shift_factors, line_rating, retention, discharge, profile, storage_bus, online_hour,
):
    hours, buses = injections.shape
    lines = shift_factors.shape[0]
    stores = retention.shape[1]
    chunk = 4 * hours
    all_hours = chunk * planes
    local_bus = storage_bus - lax.axis_index("bus") * buses
    hbm, vmem = pl.BlockSpec(memory_space=pl.ANY), pl.BlockSpec(memory_space=pltpu.VMEM)
    dma = pltpu.SemaphoreType.DMA
    bus_adjoint, stats, _ = pl.pallas_call(
        functools.partial(kernel, planes, bus_count),
        out_shape=(
            jax.ShapeDtypeStruct((hours, buses), F32),
            jax.ShapeDtypeStruct((8, stores), F32),
            jax.ShapeDtypeStruct((planes, chunk, buses), F32),
        ),
        in_specs=[hbm, hbm, hbm, vmem, vmem, vmem, vmem, vmem],
        out_specs=(hbm, vmem, hbm),
        scratch_shapes=[
            pltpu.VMEM((lines, buses), BF16),
            pltpu.VMEM((lines, buses), BF16),
            pltpu.VMEM((chunk, buses), F32),
            pltpu.VMEM((chunk, buses), BF16),
            pltpu.VMEM((chunk, buses), BF16),
            pltpu.VMEM((planes, chunk, lines), F32),
            pltpu.VMEM((planes, bus_count - 1, chunk, lines), F32),
            pltpu.VMEM((chunk, lines), BF16),
            pltpu.VMEM((chunk, lines), BF16),
            pltpu.VMEM((chunk, lines), jnp.int32),
            pltpu.VMEM((4, hours, buses), F32),
            pltpu.VMEM((planes, 2, hours, buses), F32),
            pltpu.VMEM((planes, hours, buses), F32),
            pltpu.VMEM((planes, hours, buses), F32),
            pltpu.VMEM((hours, stores), F32),
            dma((1,)),
            dma((2, planes)), dma((planes,)),
            dma((planes,)), dma((planes,)),
            dma((2, planes)), dma((2, planes)),
            dma((planes, bus_count - 1)), dma((planes, bus_count - 1)),
            dma((planes, 2)), dma((planes, 2)),
            dma((planes,)), dma((planes,)),
            dma((planes,)), dma((planes,)),
        ],
        compiler_params=pltpu.CompilerParams(
            collective_id=0, has_side_effects=True, vmem_limit_bytes=60 * 2**20
        ),
        cost_estimate=pl.CostEstimate(
            flops=12 * all_hours * lines * buses,
            bytes_accessed=4 * (lines * buses + all_hours * (buses + lines)),
            transcendentals=0,
        ),
    )(
        injections, shift_factors, line_rating, retention, discharge[None], profile,
        local_bus[None], online_hour[None],
    )
    everyone = lax.all_gather(stats, "line")
    carried = jnp.zeros((stores,), F32)
    total = jnp.zeros((stores,), F32)
    for block in reversed(range(4 * planes)):
        offset, gain, fixed, slope = (everyone[block, i] for i in range(4))
        total = total + (fixed + slope * carried)
        carried = offset + gain * carried
    return (bus_adjoint, total / math.sqrt(all_hours))


def solution(mesh):
    planes, bus_count = mesh.shape["line"] // 4, mesh.shape["bus"]
    in_specs = (
        P("line", "bus"),
        P("line", "bus"),
        P(None, "line"),
        P("line", "bus"),
        P("bus"),
        P("line", "bus"),
        P("bus"),
        P("bus"),
    )
    out_specs = (P("line", "bus"), P("bus"))
    return jax.shard_map(
        functools.partial(on_device, planes, bus_count),
        mesh=mesh, in_specs=in_specs, out_specs=out_specs, check_vma=False,
    )
```

```python
import functools
import math

import jax
import jax.numpy as jnp
from jax import lax
from jax.experimental import pallas as pl
from jax.experimental.pallas import tpu as pltpu
from jax.sharding import PartitionSpec as P

MESH = pl.DeviceIdType.MESH
F32, BF16 = jnp.float32, jnp.bfloat16


def split(value):
    high = value.astype(BF16)
    return high, (value - high.astype(F32)).astype(BF16)


def dot3(a_hi, a_lo, b_hi, b_lo, dims):
    dot = functools.partial(
        lax.dot_general, dimension_numbers=(dims, ((), ())), preferred_element_type=F32
    )
    return dot(a_hi, b_hi) + (dot(a_hi, b_lo) + dot(a_lo, b_hi))


def tile_of(width, most):
    return math.gcd(width, most)


def kernel(
    planes, bus_count,
    inj, factors, rating, retention, discharge, profile, storage_bus, online,
    out, size, gathered,
    s_hi, s_lo, stage, turned, flows, flows_in, a_hi, a_lo, limit, part,
    from_core, from_x, from_z, source, all_stats,
    local_sem,
    gz_send, gz_recv, gx_send, gx_recv, gc_send, gc_recv,
    y_send, y_recv, rc_send, rc_recv, rx_send, rx_recv, rz_send, rz_recv, st_send, st_recv,
):
    line, bus = lax.axis_index("line"), lax.axis_index("bus")
    z, x, c = line // 4, (line // 2) % 2, line % 2
    me = 2 * x + c
    hours, buses = inj.shape
    lines = factors.shape[0]
    chunk = 4 * hours

    def at(plane, column, core):
        return (plane * 4 + column * 2 + core, bus)

    sibling, across = at(z, x, 1 - c), at(z, 1 - x, c)

    def plane_of(s):
        both = jnp.minimum(z, planes - 1 - z)
        away = (s + 1) // 2
        near = jnp.where(s % 2 == 1, z - away, z + away)
        far = jnp.where(z < planes - 1 - z, s, planes - 1 - s)
        return jnp.where(s <= 2 * both, near, far)

    def rows(block):
        return pl.ds(pl.multiple_of(block * hours, hours), hours)

    def block_copy(plane, block, send, recv, target):
        ref = gathered.at[plane, rows(block)]
        return pltpu.make_async_remote_copy(
            src_ref=ref, dst_ref=ref, send_sem=send, recv_sem=recv,
            device_id=target, device_id_type=MESH,
        )

    def along_z(plane, way, target_plane):
        return block_copy(
            plane, me, gz_send.at[way, plane], gz_recv.at[plane], at(target_plane, x, c)
        )

    def to_across(plane):
        return block_copy(plane, me, gx_send.at[plane], gx_recv.at[plane], across)

    def from_across(plane):
        return block_copy(
            plane, 2 * (1 - x) + c, gx_send.at[plane], gx_recv.at[plane], across
        )

    def to_sibling(plane, k):
        block = 2 * (x if k == 0 else 1 - x) + c
        return block_copy(plane, block, gc_send.at[k, plane], gc_recv.at[k, plane], sibling)

    def from_sibling(plane, k):
        block = 2 * (x if k == 0 else 1 - x) + 1 - c
        return block_copy(plane, block, gc_send.at[k, plane], gc_recv.at[k, plane], sibling)

    def goes_up(plane):
        return (plane <= z) & (z + 1 < planes)

    def goes_down(plane):
        return (plane >= z) & (z > 0)

    def forward(s):
        plane = plane_of(s)

        @pl.when(s > 0)
        def _():
            along_z(plane, 0, z).wait_recv()

        @pl.when(goes_up(plane))
        def _():
            along_z(plane, 0, z + 1).start()

        @pl.when(goes_down(plane))
        def _():
            along_z(plane, 1, z - 1).start()

        to_across(plane).start()
        to_sibling(plane, 0).start()

    def forward_across(s):
        plane = plane_of(s)
        from_across(plane).wait_recv()
        to_sibling(plane, 1).start()

    def flow_copy(s, r):
        return pltpu.make_async_remote_copy(
            src_ref=flows.at[s], dst_ref=flows_in.at[s, r - 1],
            send_sem=y_send.at[s, r - 1], recv_sem=y_recv.at[s, r - 1],
            device_id=(line, (bus + r) % bus_count), device_id_type=MESH,
        )

    def first_product(s):
        plane = plane_of(s)
        from_sibling(plane, 0).wait_recv()
        from_sibling(plane, 1).wait_recv()
        load = pltpu.make_async_copy(gathered.at[plane], stage, local_sem.at[0])
        load.start()
        load.wait()
        width = tile_of(buses, 1024)
        turned[...] = jnp.zeros_like(turned)

        @pl.loop(0, buses // width)
        def _(n):
            here = pl.ds(pl.multiple_of(n * width, width), width)
            x_hi, x_lo = split(stage[:, here])
            turned[...] += dot3(s_hi[:, here], s_lo[:, here], x_hi, x_lo, ((1,), (1,)))

        step = tile_of(lines, 128)

        @pl.loop(0, lines // step)
        def _(n):
            here = pl.ds(pl.multiple_of(n * step, step), step)
            flows[s, :, here] = turned[here].T

        for r in range(1, bus_count):
            flow_copy(s, r).start()

    half = buses // 2

    def columns(h):
        return pl.ds(h * half, half)

    def core_copy(s, k, h):
        return pltpu.make_async_remote_copy(
            src_ref=part.at[2 * k + 1 - c, :, columns(h)],
            dst_ref=from_core.at[s, k, :, columns(h)],
            send_sem=rc_send.at[s, k, h], recv_sem=rc_recv.at[s, k, h],
            device_id=sibling, device_id_type=MESH,
        )

    def x_copy(s, h):
        return pltpu.make_async_remote_copy(
            src_ref=from_core.at[s, 1 - x, :, columns(h)],
            dst_ref=from_x.at[s, :, columns(h)],
            send_sem=rx_send.at[s, h], recv_sem=rx_recv.at[s, h],
            device_id=across, device_id_type=MESH,
        )

    def z_copy(s, h, target, slot):
        return pltpu.make_async_remote_copy(
            src_ref=from_x.at[s, :, columns(h)], dst_ref=from_z.at[slot, :, columns(h)],
            send_sem=rz_send.at[s, h], recv_sem=rz_recv.at[slot, h],
            device_id=at(target, x, c), device_id_type=MESH,
        )

    def second_product(s):
        plane = plane_of(s)
        here = pl.ds(pl.multiple_of(plane * chunk, chunk), chunk)
        load = pltpu.make_async_copy(rating.at[here], limit, local_sem.at[0])
        load.start()
        for r in range(1, bus_count):
            flow_copy(s, r).wait_recv()
        load.wait()
        step = tile_of(chunk, 32)

        @pl.loop(0, chunk // step)
        def _(i):
            here = pl.ds(pl.multiple_of(i * step, step), step)
            total = flows[s, here]
            for r in range(1, bus_count):
                total = total + flows_in[s, r - 1, here]
            bound = limit[here].astype(F32) * 0.01
            adjoint = jnp.where(
                total > bound, total - bound, jnp.where(total < -bound, total + bound, 0.0)
            )
            a_hi[here], a_lo[here] = split(adjoint)

    def second_half(s, h):
        width = tile_of(half, 512)

        @pl.loop(0, half // width)
        def _(n):
            here = pl.ds(pl.multiple_of(h * half + n * width, width), width)
            value = dot3(a_hi[...], a_lo[...], s_hi[:, here], s_lo[:, here], ((1,), (0,)))
            for block in range(4):
                part[block, :, here] = value[block * hours : (block + 1) * hours]

        for k in range(2):
            core_copy(s, k, h).start()

    def add_to(ref, other, h=None):
        step = tile_of(hours, 8)
        cols = pl.ds(0, buses) if h is None else columns(h)

        @pl.loop(0, hours // step)
        def _(i):
            here = pl.ds(pl.multiple_of(i * step, step), step)
            ref[here, cols] += other[here, cols]

    def reduce_across(s, h):
        for k in range(2):
            core_copy(s, k, h).wait_recv()
        add_to(from_core.at[s, 1 - x], part.at[2 * (1 - x) + c], h)
        x_copy(s, h).start()
        add_to(from_core.at[s, x], part.at[me], h)

    def reduce_along(s):
        for h in range(2):
            x_copy(s, h).wait_recv()
            add_to(from_x.at[s], from_core.at[s, x], h)

            @pl.when(s > 0)
            def _():
                z_copy(s, h, plane_of(s), z).start()

    def stat_copy(step, r=1):
        pair = 2 * x
        src, target = (
            (all_stats.at[z, pl.ds(me, 1)], sibling),
            (all_stats.at[z, pl.ds(pair, 2)], across),
            (all_stats.at[z], at((z + r) % planes, x, c)),
        )[step]
        return pltpu.make_async_remote_copy(
            src_ref=src, dst_ref=src,
            send_sem=st_send.at[step + r - 1], recv_sem=st_recv.at[step + r - 1],
            device_id=target, device_id_type=MESH,
        )

    def stat_arrival(step, r=1):
        plane = (z - r + planes) % planes
        ref = (
            all_stats.at[z, pl.ds(2 * x + 1 - c, 1)],
            all_stats.at[z, pl.ds(2 * (1 - x), 2)],
            all_stats.at[plane],
        )[step]
        return pltpu.make_async_remote_copy(
            src_ref=ref, dst_ref=ref,
            send_sem=st_send.at[step + r - 1], recv_sem=st_recv.at[step + r - 1],
            device_id=sibling, device_id_type=MESH,
        )

    barrier = pltpu.get_barrier_semaphore()
    mine = pltpu.make_async_copy(inj, gathered.at[z, rows(me)], local_sem.at[0])
    mine.start()
    for target in (sibling, across):
        pl.semaphore_signal(barrier, inc=1, device_id=target, device_id_type=MESH)
    for r in range(1, planes):
        pl.semaphore_signal(
            barrier, inc=1, device_id=at((z + r) % planes, x, c), device_id_type=MESH
        )
    for r in range(1, bus_count):
        pl.semaphore_signal(
            barrier, inc=1, device_id=(line, (bus + r) % bus_count), device_id_type=MESH
        )
    mine.wait()
    pl.semaphore_wait(barrier, planes + bus_count)
    forward(0)

    group = tile_of(lines, chunk)

    def factor_load(i):
        here = pl.ds(pl.multiple_of(i * group, group), group)
        return pltpu.make_async_copy(factors.at[here], stage.at[pl.ds(0, group)], local_sem.at[0])

    @pl.loop(0, lines // group)
    def _(i):
        factor_load(i).start()
        factor_load(i).wait()
        step = tile_of(group, 16)

        @pl.loop(0, group // step)
        def _(j):
            here = pl.ds(pl.multiple_of(j * step, step), step)
            there = pl.ds(pl.multiple_of(i * group + j * step, step), step)
            s_hi[there], s_lo[there] = split(stage[here])

    @pl.loop(0, planes + 3)
    def _(t):
        @pl.when(t + 1 < planes)
        def _():
            forward(t + 1)

        @pl.when(t < planes)
        def _():
            forward_across(t)
            first_product(t)

        @pl.when((t >= 2) & (t < planes + 2))
        def _():
            s = (t - 1) % planes
            second_product(s)
            second_half(s, 0)
            second_half(s, 1)
            reduce_across(s, 0)
            reduce_across(s, 1)
            for h in range(2):
                for k in range(2):
                    core_copy(s, k, h).wait_send()

        @pl.when(t >= 3)
        def _():
            reduce_along((t - 2) % planes)

    total = from_x.at[0]
    for r in range(1, planes):
        other = (z + r) % planes
        for h in range(2):
            z_copy(0, h, other, other).wait_recv()
        add_to(total, from_z.at[other])
    store = pltpu.make_async_copy(total, out, local_sem.at[0])
    store.start()

    width = tile_of(buses, 512)
    source[...] = jnp.zeros_like(source)

    @pl.loop(0, buses // width)
    def _(n):
        here = pl.ds(pl.multiple_of(n * width, width), width)
        place = lax.broadcasted_iota(jnp.int32, (width, source.shape[1]), 0)
        chosen = jnp.where(place + (bus * buses + n * width) == storage_bus[...], 1.0, 0.0).astype(BF16)
        left = total[:, here]
        for _ in range(3):
            high = left.astype(BF16)
            left = left - high.astype(F32)
            source[...] += jnp.dot(high, chosen, preferred_element_type=F32)

    def hour_back(i, carried):
        carry, gain, fixed, slope = carried
        t = hours - 1 - i
        keep = retention[pl.ds(t, 1), :]
        weight = jnp.where(line * hours + t >= online[...], profile[pl.ds(t, 1), :], 0.0)
        costate = discharge[...] * source[pl.ds(t, 1), :] + carry
        return (keep * costate, keep * gain, fixed + costate * weight, slope + gain * weight)

    all_stats[z, me] = jnp.zeros(all_stats.shape[2:], F32)
    zero = jnp.zeros((1, source.shape[1]), F32)
    done = lax.fori_loop(0, hours, hour_back, (zero, zero + 1.0, zero, zero))
    for i in range(4):
        all_stats[z, me, i : i + 1, :] = done[i]
    for step in range(2):
        stat_copy(step).start()
        stat_arrival(step).wait_recv()
    for r in range(1, planes):
        stat_copy(2, r).start()
    for r in range(1, planes):
        stat_arrival(2, r).wait_recv()

    def block_back(i, carried):
        carry, total = carried
        block = 4 * planes - 1 - i
        offset, gain, fixed, slope = (
            all_stats[block // 4, block % 4, row : row + 1, :] for row in range(4)
        )
        return (offset + gain * carry, total + (fixed + slope * carry))

    sums = lax.fori_loop(0, 4 * planes, block_back, (zero, zero))
    size[...] = sums[1] / math.sqrt(4 * planes * hours)
    for step in range(2):
        stat_copy(step).wait_send()
    for r in range(1, planes):
        stat_copy(2, r).wait_send()
    store.wait()

    @pl.loop(0, planes)
    def _(s):
        plane = plane_of(s)

        @pl.when(goes_up(plane))
        def _():
            along_z(plane, 0, z + 1).wait_send()

        @pl.when(goes_down(plane))
        def _():
            along_z(plane, 1, z - 1).wait_send()

        to_across(plane).wait_send()
        for k in range(2):
            to_sibling(plane, k).wait_send()
        for r in range(1, bus_count):
            flow_copy(s, r).wait_send()
        for h in range(2):
            x_copy(s, h).wait_send()

        @pl.when(s > 0)
        def _():
            for h in range(2):
                z_copy(s, h, plane_of(s), z).wait_send()


def on_device(
    planes, bus_count,
    injections, shift_factors, line_rating, retention, discharge, profile, storage_bus, online_hour,
):
    hours, buses = injections.shape
    lines = shift_factors.shape[0]
    stores = retention.shape[1]
    chunk = 4 * hours
    all_hours = chunk * planes
    hbm, vmem = pl.BlockSpec(memory_space=pl.ANY), pl.BlockSpec(memory_space=pltpu.VMEM)
    dma = pltpu.SemaphoreType.DMA
    bus_adjoint, size_grad, _ = pl.pallas_call(
        functools.partial(kernel, planes, bus_count),
        out_shape=(
            jax.ShapeDtypeStruct((hours, buses), F32),
            jax.ShapeDtypeStruct((1, stores), F32),
            jax.ShapeDtypeStruct((planes, chunk, buses), F32),
        ),
        in_specs=[hbm, hbm, hbm, vmem, vmem, vmem, vmem, vmem],
        out_specs=(hbm, vmem, hbm),
        scratch_shapes=[
            pltpu.VMEM((lines, buses), BF16),
            pltpu.VMEM((lines, buses), BF16),
            pltpu.VMEM((chunk, buses), F32),
            pltpu.VMEM((lines, chunk), F32),
            pltpu.VMEM((planes, chunk, lines), F32),
            pltpu.VMEM((planes, bus_count - 1, chunk, lines), F32),
            pltpu.VMEM((chunk, lines), BF16),
            pltpu.VMEM((chunk, lines), BF16),
            pltpu.VMEM((chunk, lines), jnp.int32),
            pltpu.VMEM((4, hours, buses), F32),
            pltpu.VMEM((planes, 2, hours, buses), F32),
            pltpu.VMEM((planes, hours, buses), F32),
            pltpu.VMEM((planes, hours, buses), F32),
            pltpu.VMEM((hours, stores), F32),
            pltpu.VMEM((planes, 4, 8, stores), F32),
            dma((1,)),
            dma((2, planes)), dma((planes,)),
            dma((planes,)), dma((planes,)),
            dma((2, planes)), dma((2, planes)),
            dma((planes, bus_count - 1)), dma((planes, bus_count - 1)),
            dma((planes, 2, 2)), dma((planes, 2, 2)),
            dma((planes, 2)), dma((planes, 2)),
            dma((planes, 2)), dma((planes, 2)),
            dma((planes + 1,)), dma((planes + 1,)),
        ],
        compiler_params=pltpu.CompilerParams(
            collective_id=0, has_side_effects=True, vmem_limit_bytes=60 * 2**20
        ),
        cost_estimate=pl.CostEstimate(
            flops=12 * all_hours * lines * buses,
            bytes_accessed=4 * (lines * buses + all_hours * (buses + lines)),
            transcendentals=0,
        ),
    )(
        injections, shift_factors, line_rating, retention, discharge[None], profile,
        storage_bus[None], online_hour[None],
    )
    return (bus_adjoint, size_grad[0])


def solution(mesh):
    planes, bus_count = mesh.shape["line"] // 4, mesh.shape["bus"]
    in_specs = (
        P("line", "bus"),
        P("line", "bus"),
        P(None, "line"),
        P("line", "bus"),
        P("bus"),
        P("line", "bus"),
        P("bus"),
        P("bus"),
    )
    out_specs = (P("line", "bus"), P("bus"))
    return jax.shard_map(
        functools.partial(on_device, planes, bus_count),
        mesh=mesh, in_specs=in_specs, out_specs=out_specs, check_vma=False,
    )
```

```python
import functools
import math

import jax
import jax.numpy as jnp
from jax import lax
from jax.experimental import pallas as pl
from jax.experimental.pallas import tpu as pltpu
from jax.sharding import PartitionSpec as P

MESH = pl.DeviceIdType.MESH
F32, BF16 = jnp.float32, jnp.bfloat16


def split(value):
    high = value.astype(BF16)
    return high, (value - high.astype(F32)).astype(BF16)


def dot3(a_hi, a_lo, b_hi, b_lo, dims):
    dot = functools.partial(
        lax.dot_general, dimension_numbers=(dims, ((), ())), preferred_element_type=F32
    )
    return dot(a_hi, b_hi) + (dot(a_hi, b_lo) + dot(a_lo, b_hi))


def tile_of(width, most):
    return math.gcd(width, most)


def kernel(
    planes, bus_count,
    inj, factors, rating, retention, discharge, profile, storage_bus, online,
    out, size, gathered,
    s_hi, s_lo, stage, turned, flows, flows_in, a_hi, a_lo, limit, part,
    from_core, from_x, from_z, source, all_stats,
    local_sem,
    gz_send, gz_recv, gx_send, gx_recv, gc_send, gc_recv,
    y_send, y_recv, rc_send, rc_recv, rx_send, rx_recv, rz_send, rz_recv, st_send, st_recv,
):
    line, bus = lax.axis_index("line"), lax.axis_index("bus")
    z, x, c = line // 4, (line // 2) % 2, line % 2
    me = 2 * x + c
    hours, buses = inj.shape
    lines = factors.shape[0]
    chunk = 4 * hours

    def at(plane, column, core):
        return (plane * 4 + column * 2 + core, bus)

    sibling, across = at(z, x, 1 - c), at(z, 1 - x, c)

    def plane_of(s):
        above = planes - 1 - z
        up = jnp.where(s <= above, z + s, z - (s - above))
        down = jnp.where(s <= z, z - s, s)
        return jnp.where(z <= above, up, down)

    def rows(block):
        return pl.ds(pl.multiple_of(block * hours, hours), hours)

    def block_copy(plane, block, send, recv, target):
        ref = gathered.at[plane, rows(block)]
        return pltpu.make_async_remote_copy(
            src_ref=ref, dst_ref=ref, send_sem=send, recv_sem=recv,
            device_id=target, device_id_type=MESH,
        )

    def along_z(plane, way, target_plane):
        return block_copy(
            plane, me, gz_send.at[way, plane], gz_recv.at[plane], at(target_plane, x, c)
        )

    def to_across(plane):
        return block_copy(plane, me, gx_send.at[plane], gx_recv.at[plane], across)

    def from_across(plane):
        return block_copy(
            plane, 2 * (1 - x) + c, gx_send.at[plane], gx_recv.at[plane], across
        )

    def to_sibling(plane, k):
        block = 2 * (x if k == 0 else 1 - x) + c
        return block_copy(plane, block, gc_send.at[k, plane], gc_recv.at[k, plane], sibling)

    def from_sibling(plane, k):
        block = 2 * (x if k == 0 else 1 - x) + 1 - c
        return block_copy(plane, block, gc_send.at[k, plane], gc_recv.at[k, plane], sibling)

    def goes_up(plane):
        return (plane <= z) & (z + 1 < planes)

    def goes_down(plane):
        return (plane >= z) & (z > 0)

    def pass_on(plane):
        @pl.when(plane != z)
        def _():
            along_z(plane, 0, z).wait_recv()

        @pl.when(goes_up(plane))
        def _():
            along_z(plane, 0, z + 1).start()

        @pl.when(goes_down(plane))
        def _():
            along_z(plane, 1, z - 1).start()

        to_sibling(plane, 0).start()

    def pass_on_at(distance):
        @pl.when(z - distance >= 0)
        def _():
            pass_on(z - distance)

        @pl.when(z + distance < planes)
        def _():
            pass_on(z + distance)

    def forward_across(s):
        plane = plane_of(s)
        from_across(plane).wait_recv()
        to_sibling(plane, 1).start()

    def flow_copy(s, r):
        return pltpu.make_async_remote_copy(
            src_ref=flows.at[s], dst_ref=flows_in.at[s, r - 1],
            send_sem=y_send.at[s, r - 1], recv_sem=y_recv.at[s, r - 1],
            device_id=(line, (bus + r) % bus_count), device_id_type=MESH,
        )

    def first_product(s):
        plane = plane_of(s)
        from_sibling(plane, 0).wait_recv()
        from_sibling(plane, 1).wait_recv()
        load = pltpu.make_async_copy(gathered.at[plane], stage, local_sem.at[0])
        load.start()
        load.wait()
        width = tile_of(buses, 1024)
        turned[...] = jnp.zeros_like(turned)

        @pl.loop(0, buses // width)
        def _(n):
            here = pl.ds(pl.multiple_of(n * width, width), width)
            x_hi, x_lo = split(stage[:, here])
            turned[...] += dot3(s_hi[:, here], s_lo[:, here], x_hi, x_lo, ((1,), (1,)))

        step = tile_of(lines, 128)

        @pl.loop(0, lines // step)
        def _(n):
            here = pl.ds(pl.multiple_of(n * step, step), step)
            flows[s, :, here] = turned[here].T

        for r in range(1, bus_count):
            flow_copy(s, r).start()

    half = buses // 2

    def columns(h):
        return pl.ds(h * half, half)

    def core_copy(s, k, h):
        return pltpu.make_async_remote_copy(
            src_ref=part.at[2 * k + 1 - c, :, columns(h)],
            dst_ref=from_core.at[s, k, :, columns(h)],
            send_sem=rc_send.at[s, k, h], recv_sem=rc_recv.at[s, k, h],
            device_id=sibling, device_id_type=MESH,
        )

    def x_copy(s, h):
        return pltpu.make_async_remote_copy(
            src_ref=from_core.at[s, 1 - x, :, columns(h)],
            dst_ref=from_x.at[s, :, columns(h)],
            send_sem=rx_send.at[s, h], recv_sem=rx_recv.at[s, h],
            device_id=across, device_id_type=MESH,
        )

    def z_copy(s, h, target, slot):
        return pltpu.make_async_remote_copy(
            src_ref=from_x.at[s, :, columns(h)], dst_ref=from_z.at[slot, :, columns(h)],
            send_sem=rz_send.at[s, h], recv_sem=rz_recv.at[slot, h],
            device_id=at(target, x, c), device_id_type=MESH,
        )

    def second_product(s):
        plane = plane_of(s)
        here = pl.ds(pl.multiple_of(plane * chunk, chunk), chunk)
        load = pltpu.make_async_copy(rating.at[here], limit, local_sem.at[0])
        load.start()
        for r in range(1, bus_count):
            flow_copy(s, r).wait_recv()
        load.wait()
        step = tile_of(chunk, 32)

        @pl.loop(0, chunk // step)
        def _(i):
            here = pl.ds(pl.multiple_of(i * step, step), step)
            total = flows[s, here]
            for r in range(1, bus_count):
                total = total + flows_in[s, r - 1, here]
            bound = limit[here].astype(F32) * 0.01
            adjoint = jnp.where(
                total > bound, total - bound, jnp.where(total < -bound, total + bound, 0.0)
            )
            a_hi[here], a_lo[here] = split(adjoint)

    def second_half(s, h):
        width = tile_of(half, 512)

        @pl.loop(0, half // width)
        def _(n):
            here = pl.ds(pl.multiple_of(h * half + n * width, width), width)
            value = dot3(a_hi[...], a_lo[...], s_hi[:, here], s_lo[:, here], ((1,), (0,)))
            for block in range(4):
                part[block, :, here] = value[block * hours : (block + 1) * hours]

        for k in range(2):
            core_copy(s, k, h).start()

    def add_to(ref, other, h=None):
        step = tile_of(hours, 8)
        cols = pl.ds(0, buses) if h is None else columns(h)

        @pl.loop(0, hours // step)
        def _(i):
            here = pl.ds(pl.multiple_of(i * step, step), step)
            ref[here, cols] += other[here, cols]

    def reduce_across(s, h):
        for k in range(2):
            core_copy(s, k, h).wait_recv()
        add_to(from_core.at[s, 1 - x], part.at[2 * (1 - x) + c], h)
        x_copy(s, h).start()
        add_to(from_core.at[s, x], part.at[me], h)

    def reduce_along(s):
        for h in range(2):
            x_copy(s, h).wait_recv()
            add_to(from_x.at[s], from_core.at[s, x], h)

            @pl.when(s > 0)
            def _():
                z_copy(s, h, plane_of(s), z).start()

    def stat_copy(step, r=1):
        pair = 2 * x
        src, target = (
            (all_stats.at[z, pl.ds(me, 1)], sibling),
            (all_stats.at[z, pl.ds(pair, 2)], across),
            (all_stats.at[z], at((z + r) % planes, x, c)),
        )[step]
        return pltpu.make_async_remote_copy(
            src_ref=src, dst_ref=src,
            send_sem=st_send.at[step + r - 1], recv_sem=st_recv.at[step + r - 1],
            device_id=target, device_id_type=MESH,
        )

    def stat_arrival(step, r=1):
        plane = (z - r + planes) % planes
        ref = (
            all_stats.at[z, pl.ds(2 * x + 1 - c, 1)],
            all_stats.at[z, pl.ds(2 * (1 - x), 2)],
            all_stats.at[plane],
        )[step]
        return pltpu.make_async_remote_copy(
            src_ref=ref, dst_ref=ref,
            send_sem=st_send.at[step + r - 1], recv_sem=st_recv.at[step + r - 1],
            device_id=sibling, device_id_type=MESH,
        )

    barrier = pltpu.get_barrier_semaphore()
    mine = pltpu.make_async_copy(inj, gathered.at[z, rows(me)], local_sem.at[0])
    mine.start()
    for target in (sibling, across):
        pl.semaphore_signal(barrier, inc=1, device_id=target, device_id_type=MESH)
    for r in range(1, planes):
        pl.semaphore_signal(
            barrier, inc=1, device_id=at((z + r) % planes, x, c), device_id_type=MESH
        )
    for r in range(1, bus_count):
        pl.semaphore_signal(
            barrier, inc=1, device_id=(line, (bus + r) % bus_count), device_id_type=MESH
        )
    mine.wait()
    pl.semaphore_wait(barrier, planes + bus_count)
    pass_on(z)
    to_across(z).start()

    group = tile_of(lines, chunk)

    def factor_load(i):
        here = pl.ds(pl.multiple_of(i * group, group), group)
        return pltpu.make_async_copy(factors.at[here], stage.at[pl.ds(0, group)], local_sem.at[0])

    @pl.loop(0, lines // group)
    def _(i):
        factor_load(i).start()
        factor_load(i).wait()
        step = tile_of(group, 16)

        @pl.loop(0, group // step)
        def _(j):
            here = pl.ds(pl.multiple_of(j * step, step), step)
            there = pl.ds(pl.multiple_of(i * group + j * step, step), step)
            s_hi[there], s_lo[there] = split(stage[here])

    @pl.loop(0, planes + 3)
    def _(t):
        @pl.when(t + 1 < planes)
        def _():
            pass_on_at(t + 1)
            to_across(plane_of(t + 1)).start()

        @pl.when(t < planes)
        def _():
            forward_across(t)
            first_product(t)

        @pl.when((t >= 2) & (t < planes + 2))
        def _():
            s = (t - 1) % planes
            second_product(s)
            second_half(s, 0)
            second_half(s, 1)
            reduce_across(s, 0)
            reduce_across(s, 1)
            for h in range(2):
                for k in range(2):
                    core_copy(s, k, h).wait_send()

        @pl.when(t >= 3)
        def _():
            reduce_along((t - 2) % planes)

    total = from_x.at[0]
    for r in range(1, planes):
        other = (z + r) % planes
        for h in range(2):
            z_copy(0, h, other, other).wait_recv()
        add_to(total, from_z.at[other])
    store = pltpu.make_async_copy(total, out, local_sem.at[0])
    store.start()

    width = tile_of(buses, 512)
    source[...] = jnp.zeros_like(source)

    @pl.loop(0, buses // width)
    def _(n):
        here = pl.ds(pl.multiple_of(n * width, width), width)
        place = lax.broadcasted_iota(jnp.int32, (width, source.shape[1]), 0)
        chosen = jnp.where(place + (bus * buses + n * width) == storage_bus[...], 1.0, 0.0).astype(BF16)
        left = total[:, here]
        for _ in range(3):
            high = left.astype(BF16)
            left = left - high.astype(F32)
            source[...] += jnp.dot(high, chosen, preferred_element_type=F32)

    def hour_back(i, carried):
        carry, gain, fixed, slope = carried
        t = hours - 1 - i
        keep = retention[pl.ds(t, 1), :]
        weight = jnp.where(line * hours + t >= online[...], profile[pl.ds(t, 1), :], 0.0)
        costate = discharge[...] * source[pl.ds(t, 1), :] + carry
        return (keep * costate, keep * gain, fixed + costate * weight, slope + gain * weight)

    all_stats[z, me] = jnp.zeros(all_stats.shape[2:], F32)
    zero = jnp.zeros((1, source.shape[1]), F32)
    done = lax.fori_loop(0, hours, hour_back, (zero, zero + 1.0, zero, zero))
    for i in range(4):
        all_stats[z, me, i : i + 1, :] = done[i]
    for step in range(2):
        stat_copy(step).start()
        stat_arrival(step).wait_recv()
    for r in range(1, planes):
        stat_copy(2, r).start()
    for r in range(1, planes):
        stat_arrival(2, r).wait_recv()

    def block_back(i, carried):
        carry, total = carried
        block = 4 * planes - 1 - i
        offset, gain, fixed, slope = (
            all_stats[block // 4, block % 4, row : row + 1, :] for row in range(4)
        )
        return (offset + gain * carry, total + (fixed + slope * carry))

    sums = lax.fori_loop(0, 4 * planes, block_back, (zero, zero))
    size[...] = sums[1] / math.sqrt(4 * planes * hours)
    for step in range(2):
        stat_copy(step).wait_send()
    for r in range(1, planes):
        stat_copy(2, r).wait_send()
    store.wait()

    @pl.loop(0, planes)
    def _(s):
        plane = plane_of(s)

        @pl.when(goes_up(plane))
        def _():
            along_z(plane, 0, z + 1).wait_send()

        @pl.when(goes_down(plane))
        def _():
            along_z(plane, 1, z - 1).wait_send()

        to_across(plane).wait_send()
        for k in range(2):
            to_sibling(plane, k).wait_send()
        for r in range(1, bus_count):
            flow_copy(s, r).wait_send()
        for h in range(2):
            x_copy(s, h).wait_send()

        @pl.when(s > 0)
        def _():
            for h in range(2):
                z_copy(s, h, plane_of(s), z).wait_send()


def on_device(
    planes, bus_count,
    injections, shift_factors, line_rating, retention, discharge, profile, storage_bus, online_hour,
):
    hours, buses = injections.shape
    lines = shift_factors.shape[0]
    stores = retention.shape[1]
    chunk = 4 * hours
    all_hours = chunk * planes
    hbm, vmem = pl.BlockSpec(memory_space=pl.ANY), pl.BlockSpec(memory_space=pltpu.VMEM)
    dma = pltpu.SemaphoreType.DMA
    bus_adjoint, size_grad, _ = pl.pallas_call(
        functools.partial(kernel, planes, bus_count),
        out_shape=(
            jax.ShapeDtypeStruct((hours, buses), F32),
            jax.ShapeDtypeStruct((1, stores), F32),
            jax.ShapeDtypeStruct((planes, chunk, buses), F32),
        ),
        in_specs=[hbm, hbm, hbm, vmem, vmem, vmem, vmem, vmem],
        out_specs=(hbm, vmem, hbm),
        scratch_shapes=[
            pltpu.VMEM((lines, buses), BF16),
            pltpu.VMEM((lines, buses), BF16),
            pltpu.VMEM((chunk, buses), F32),
            pltpu.VMEM((lines, chunk), F32),
            pltpu.VMEM((planes, chunk, lines), F32),
            pltpu.VMEM((planes, bus_count - 1, chunk, lines), F32),
            pltpu.VMEM((chunk, lines), BF16),
            pltpu.VMEM((chunk, lines), BF16),
            pltpu.VMEM((chunk, lines), jnp.int32),
            pltpu.VMEM((4, hours, buses), F32),
            pltpu.VMEM((planes, 2, hours, buses), F32),
            pltpu.VMEM((planes, hours, buses), F32),
            pltpu.VMEM((planes, hours, buses), F32),
            pltpu.VMEM((hours, stores), F32),
            pltpu.VMEM((planes, 4, 8, stores), F32),
            dma((1,)),
            dma((2, planes)), dma((planes,)),
            dma((planes,)), dma((planes,)),
            dma((2, planes)), dma((2, planes)),
            dma((planes, bus_count - 1)), dma((planes, bus_count - 1)),
            dma((planes, 2, 2)), dma((planes, 2, 2)),
            dma((planes, 2)), dma((planes, 2)),
            dma((planes, 2)), dma((planes, 2)),
            dma((planes + 1,)), dma((planes + 1,)),
        ],
        compiler_params=pltpu.CompilerParams(
            collective_id=0, has_side_effects=True, vmem_limit_bytes=60 * 2**20
        ),
        cost_estimate=pl.CostEstimate(
            flops=12 * all_hours * lines * buses,
            bytes_accessed=4 * (lines * buses + all_hours * (buses + lines)),
            transcendentals=0,
        ),
    )(
        injections, shift_factors, line_rating, retention, discharge[None], profile,
        storage_bus[None], online_hour[None],
    )
    return (bus_adjoint, size_grad[0])


def solution(mesh):
    planes, bus_count = mesh.shape["line"] // 4, mesh.shape["bus"]
    in_specs = (
        P("line", "bus"),
        P("line", "bus"),
        P(None, "line"),
        P("line", "bus"),
        P("bus"),
        P("line", "bus"),
        P("bus"),
        P("bus"),
    )
    out_specs = (P("line", "bus"), P("bus"))
    return jax.shard_map(
        functools.partial(on_device, planes, bus_count),
        mesh=mesh, in_specs=in_specs, out_specs=out_specs, check_vma=False,
    )
```

```python
import functools
import math

import jax
import jax.numpy as jnp
from jax import lax
from jax.experimental import pallas as pl
from jax.experimental.pallas import tpu as pltpu
from jax.sharding import PartitionSpec as P

MESH = pl.DeviceIdType.MESH
F32, BF16 = jnp.float32, jnp.bfloat16


def split(value):
    high = value.astype(BF16)
    return high, (value - high.astype(F32)).astype(BF16)


def dot(a, b, dims):
    return lax.dot_general(a, b, (dims, ((), ())), preferred_element_type=F32)


def tile_of(width, most):
    return math.gcd(width, most)


def kernel(
    planes, bus_count,
    inj, factors, rating, retention, discharge, profile, storage_bus, online,
    out, size, gathered,
    s_hi, s_lo, stage, turned, flows, flows_in, adjoint, limit, part,
    from_core, from_x, from_z, source, all_stats,
    local_sem,
    gz_send, gz_recv, gx_send, gx_recv, gc_send, gc_recv,
    y_send, y_recv, rc_send, rc_recv, rx_send, rx_recv, rz_send, rz_recv, st_send, st_recv,
):
    line, bus = lax.axis_index("line"), lax.axis_index("bus")
    z, x, c = line // 4, (line // 2) % 2, line % 2
    me = 2 * x + c
    hours, buses = inj.shape
    lines = factors.shape[0]
    chunk = 4 * hours

    def at(plane, column, core):
        return (plane * 4 + column * 2 + core, bus)

    sibling, across = at(z, x, 1 - c), at(z, 1 - x, c)

    def plane_of(s):
        above = planes - 1 - z
        up = jnp.where(s <= above, z + s, z - (s - above))
        down = jnp.where(s <= z, z - s, s)
        return jnp.where(z <= above, up, down)

    def rows(block):
        return pl.ds(pl.multiple_of(block * hours, hours), hours)

    def block_copy(plane, block, send, recv, target):
        ref = gathered.at[plane, rows(block)]
        return pltpu.make_async_remote_copy(
            src_ref=ref, dst_ref=ref, send_sem=send, recv_sem=recv,
            device_id=target, device_id_type=MESH,
        )

    def along_z(plane, way, target_plane):
        return block_copy(
            plane, me, gz_send.at[way, plane], gz_recv.at[plane], at(target_plane, x, c)
        )

    def to_across(plane):
        return block_copy(plane, me, gx_send.at[plane], gx_recv.at[plane], across)

    def from_across(plane):
        return block_copy(
            plane, 2 * (1 - x) + c, gx_send.at[plane], gx_recv.at[plane], across
        )

    def to_sibling(plane, k):
        block = 2 * (x if k == 0 else 1 - x) + c
        return block_copy(plane, block, gc_send.at[k, plane], gc_recv.at[k, plane], sibling)

    def from_sibling(plane, k):
        block = 2 * (x if k == 0 else 1 - x) + 1 - c
        return block_copy(plane, block, gc_send.at[k, plane], gc_recv.at[k, plane], sibling)

    def goes_up(plane):
        return (plane <= z) & (z + 1 < planes)

    def goes_down(plane):
        return (plane >= z) & (z > 0)

    def pass_on(plane):
        @pl.when(plane != z)
        def _():
            along_z(plane, 0, z).wait_recv()

        @pl.when(goes_up(plane))
        def _():
            along_z(plane, 0, z + 1).start()

        @pl.when(goes_down(plane))
        def _():
            along_z(plane, 1, z - 1).start()

        to_sibling(plane, 0).start()

    def pass_on_at(distance):
        @pl.when(z - distance >= 0)
        def _():
            pass_on(z - distance)

        @pl.when(z + distance < planes)
        def _():
            pass_on(z + distance)

    def forward_across(s):
        plane = plane_of(s)
        from_across(plane).wait_recv()
        to_sibling(plane, 1).start()

    def flow_copy(s, r):
        return pltpu.make_async_remote_copy(
            src_ref=flows.at[s], dst_ref=flows_in.at[s, r - 1],
            send_sem=y_send.at[s, r - 1], recv_sem=y_recv.at[s, r - 1],
            device_id=(line, (bus + r) % bus_count), device_id_type=MESH,
        )

    def first_product(s):
        plane = plane_of(s)
        from_sibling(plane, 0).wait_recv()
        from_sibling(plane, 1).wait_recv()
        load = pltpu.make_async_copy(gathered.at[plane], stage, local_sem.at[0])
        load.start()
        load.wait()
        width = tile_of(buses, 1024)
        turned[...] = jnp.zeros_like(turned)

        @pl.loop(0, buses // width)
        def _(n):
            here = pl.ds(pl.multiple_of(n * width, width), width)
            x_hi, x_lo = split(stage[:, here])
            both = dot(s_hi[:, here], jnp.concatenate([x_hi, x_lo], axis=0), ((1,), (1,)))
            rest = dot(s_lo[:, here], x_hi, ((1,), (1,)))
            turned[...] += both[:, :chunk] + (both[:, chunk:] + rest)

        step = tile_of(lines, 128)

        @pl.loop(0, lines // step)
        def _(n):
            here = pl.ds(pl.multiple_of(n * step, step), step)
            flows[s, :, here] = turned[here].T

        for r in range(1, bus_count):
            flow_copy(s, r).start()

    half = buses // 2

    def columns(h):
        return pl.ds(h * half, half)

    def core_copy(s, k, h):
        return pltpu.make_async_remote_copy(
            src_ref=part.at[2 * k + 1 - c, :, columns(h)],
            dst_ref=from_core.at[s, k, :, columns(h)],
            send_sem=rc_send.at[s, k, h], recv_sem=rc_recv.at[s, k, h],
            device_id=sibling, device_id_type=MESH,
        )

    def x_copy(s, h):
        return pltpu.make_async_remote_copy(
            src_ref=from_core.at[s, 1 - x, :, columns(h)],
            dst_ref=from_x.at[s, :, columns(h)],
            send_sem=rx_send.at[s, h], recv_sem=rx_recv.at[s, h],
            device_id=across, device_id_type=MESH,
        )

    def z_copy(s, h, target, slot):
        return pltpu.make_async_remote_copy(
            src_ref=from_x.at[s, :, columns(h)], dst_ref=from_z.at[slot, :, columns(h)],
            send_sem=rz_send.at[s, h], recv_sem=rz_recv.at[slot, h],
            device_id=at(target, x, c), device_id_type=MESH,
        )

    def second_product(s):
        plane = plane_of(s)
        here = pl.ds(pl.multiple_of(plane * chunk, chunk), chunk)
        load = pltpu.make_async_copy(rating.at[here], limit, local_sem.at[0])
        load.start()
        for r in range(1, bus_count):
            flow_copy(s, r).wait_recv()
        load.wait()
        step = tile_of(chunk, 32)

        @pl.loop(0, chunk // step)
        def _(i):
            here = pl.ds(pl.multiple_of(i * step, step), step)
            total = flows[s, here]
            for r in range(1, bus_count):
                total = total + flows_in[s, r - 1, here]
            bound = limit[here].astype(F32) * 0.01
            excess = jnp.where(
                total > bound, total - bound, jnp.where(total < -bound, total + bound, 0.0)
            )
            below = pl.ds(pl.multiple_of(chunk + i * step, step), step)
            adjoint[here], adjoint[below] = split(excess)

    def second_half(s, h):
        width = tile_of(half, 512)

        @pl.loop(0, half // width)
        def _(n):
            here = pl.ds(pl.multiple_of(h * half + n * width, width), width)
            both = dot(adjoint[...], s_hi[:, here], ((1,), (0,)))
            rest = dot(adjoint[:chunk], s_lo[:, here], ((1,), (0,)))
            value = both[:chunk] + (both[chunk:] + rest)
            for block in range(4):
                part[block, :, here] = value[block * hours : (block + 1) * hours]

        for k in range(2):
            core_copy(s, k, h).start()

    def add_to(ref, other, h=None):
        step = tile_of(hours, 8)
        cols = pl.ds(0, buses) if h is None else columns(h)

        @pl.loop(0, hours // step)
        def _(i):
            here = pl.ds(pl.multiple_of(i * step, step), step)
            ref[here, cols] += other[here, cols]

    def reduce_across(s, h):
        for k in range(2):
            core_copy(s, k, h).wait_recv()
        add_to(from_core.at[s, 1 - x], part.at[2 * (1 - x) + c], h)
        x_copy(s, h).start()
        add_to(from_core.at[s, x], part.at[me], h)

    def reduce_along(s):
        for h in range(2):
            x_copy(s, h).wait_recv()
            add_to(from_x.at[s], from_core.at[s, x], h)

            @pl.when(s > 0)
            def _():
                z_copy(s, h, plane_of(s), z).start()

    def stat_copy(step, r=1):
        pair = 2 * x
        src, target = (
            (all_stats.at[z, pl.ds(me, 1)], sibling),
            (all_stats.at[z, pl.ds(pair, 2)], across),
            (all_stats.at[z], at((z + r) % planes, x, c)),
        )[step]
        return pltpu.make_async_remote_copy(
            src_ref=src, dst_ref=src,
            send_sem=st_send.at[step + r - 1], recv_sem=st_recv.at[step + r - 1],
            device_id=target, device_id_type=MESH,
        )

    def stat_arrival(step, r=1):
        plane = (z - r + planes) % planes
        ref = (
            all_stats.at[z, pl.ds(2 * x + 1 - c, 1)],
            all_stats.at[z, pl.ds(2 * (1 - x), 2)],
            all_stats.at[plane],
        )[step]
        return pltpu.make_async_remote_copy(
            src_ref=ref, dst_ref=ref,
            send_sem=st_send.at[step + r - 1], recv_sem=st_recv.at[step + r - 1],
            device_id=sibling, device_id_type=MESH,
        )

    barrier = pltpu.get_barrier_semaphore()
    mine = pltpu.make_async_copy(inj, gathered.at[z, rows(me)], local_sem.at[0])
    mine.start()
    for target in (sibling, across):
        pl.semaphore_signal(barrier, inc=1, device_id=target, device_id_type=MESH)
    for r in range(1, planes):
        pl.semaphore_signal(
            barrier, inc=1, device_id=at((z + r) % planes, x, c), device_id_type=MESH
        )
    for r in range(1, bus_count):
        pl.semaphore_signal(
            barrier, inc=1, device_id=(line, (bus + r) % bus_count), device_id_type=MESH
        )
    mine.wait()
    pl.semaphore_wait(barrier, planes + bus_count)
    pass_on(z)
    to_across(z).start()

    group = tile_of(lines, chunk)

    def factor_load(i):
        here = pl.ds(pl.multiple_of(i * group, group), group)
        return pltpu.make_async_copy(factors.at[here], stage.at[pl.ds(0, group)], local_sem.at[0])

    @pl.loop(0, lines // group)
    def _(i):
        factor_load(i).start()
        factor_load(i).wait()
        step = tile_of(group, 16)

        @pl.loop(0, group // step)
        def _(j):
            here = pl.ds(pl.multiple_of(j * step, step), step)
            there = pl.ds(pl.multiple_of(i * group + j * step, step), step)
            s_hi[there], s_lo[there] = split(stage[here])

    @pl.loop(0, planes + 2)
    def _(t):
        @pl.when(t + 1 < planes)
        def _():
            pass_on_at(t + 1)
            to_across(plane_of(t + 1)).start()

        @pl.when(t < planes)
        def _():
            forward_across(t)
            first_product(t)

        @pl.when((t >= 1) & (t < planes + 1))
        def _():
            s = t - 1
            second_product(s)
            second_half(s, 0)
            second_half(s, 1)
            reduce_across(s, 0)
            reduce_across(s, 1)
            for h in range(2):
                for k in range(2):
                    core_copy(s, k, h).wait_send()

        @pl.when(t >= 2)
        def _():
            reduce_along(t - 2)

    total = from_x.at[0]
    for r in range(1, planes):
        other = (z + r) % planes
        for h in range(2):
            z_copy(0, h, other, other).wait_recv()
        add_to(total, from_z.at[other])
    store = pltpu.make_async_copy(total, out, local_sem.at[0])
    store.start()

    width = tile_of(buses, 512)
    source[...] = jnp.zeros_like(source)

    @pl.loop(0, buses // width)
    def _(n):
        here = pl.ds(pl.multiple_of(n * width, width), width)
        place = lax.broadcasted_iota(jnp.int32, (width, source.shape[1]), 0)
        chosen = jnp.where(place + (bus * buses + n * width) == storage_bus[...], 1.0, 0.0).astype(BF16)
        left = total[:, here]
        for _ in range(3):
            high = left.astype(BF16)
            left = left - high.astype(F32)
            source[...] += jnp.dot(high, chosen, preferred_element_type=F32)

    def hour_back(i, carried):
        carry, gain, fixed, slope = carried
        t = hours - 1 - i
        keep = retention[pl.ds(t, 1), :]
        weight = jnp.where(line * hours + t >= online[...], profile[pl.ds(t, 1), :], 0.0)
        costate = discharge[...] * source[pl.ds(t, 1), :] + carry
        return (keep * costate, keep * gain, fixed + costate * weight, slope + gain * weight)

    all_stats[z, me] = jnp.zeros(all_stats.shape[2:], F32)
    zero = jnp.zeros((1, source.shape[1]), F32)
    done = lax.fori_loop(0, hours, hour_back, (zero, zero + 1.0, zero, zero))
    for i in range(4):
        all_stats[z, me, i : i + 1, :] = done[i]
    for step in range(2):
        stat_copy(step).start()
        stat_arrival(step).wait_recv()
    for r in range(1, planes):
        stat_copy(2, r).start()
    for r in range(1, planes):
        stat_arrival(2, r).wait_recv()

    def block_back(i, carried):
        carry, total = carried
        block = 4 * planes - 1 - i
        offset, gain, fixed, slope = (
            all_stats[block // 4, block % 4, row : row + 1, :] for row in range(4)
        )
        return (offset + gain * carry, total + (fixed + slope * carry))

    sums = lax.fori_loop(0, 4 * planes, block_back, (zero, zero))
    size[...] = sums[1] / math.sqrt(4 * planes * hours)
    for step in range(2):
        stat_copy(step).wait_send()
    for r in range(1, planes):
        stat_copy(2, r).wait_send()
    store.wait()

    @pl.loop(0, planes)
    def _(s):
        plane = plane_of(s)

        @pl.when(goes_up(plane))
        def _():
            along_z(plane, 0, z + 1).wait_send()

        @pl.when(goes_down(plane))
        def _():
            along_z(plane, 1, z - 1).wait_send()

        to_across(plane).wait_send()
        for k in range(2):
            to_sibling(plane, k).wait_send()
        for r in range(1, bus_count):
            flow_copy(s, r).wait_send()
        for h in range(2):
            x_copy(s, h).wait_send()

        @pl.when(s > 0)
        def _():
            for h in range(2):
                z_copy(s, h, plane_of(s), z).wait_send()


def on_device(
    planes, bus_count,
    injections, shift_factors, line_rating, retention, discharge, profile, storage_bus, online_hour,
):
    hours, buses = injections.shape
    lines = shift_factors.shape[0]
    stores = retention.shape[1]
    chunk = 4 * hours
    all_hours = chunk * planes
    hbm, vmem = pl.BlockSpec(memory_space=pl.ANY), pl.BlockSpec(memory_space=pltpu.VMEM)
    dma = pltpu.SemaphoreType.DMA
    bus_adjoint, size_grad, _ = pl.pallas_call(
        functools.partial(kernel, planes, bus_count),
        out_shape=(
            jax.ShapeDtypeStruct((hours, buses), F32),
            jax.ShapeDtypeStruct((1, stores), F32),
            jax.ShapeDtypeStruct((planes, chunk, buses), F32),
        ),
        in_specs=[hbm, hbm, hbm, vmem, vmem, vmem, vmem, vmem],
        out_specs=(hbm, vmem, hbm),
        scratch_shapes=[
            pltpu.VMEM((lines, buses), BF16),
            pltpu.VMEM((lines, buses), BF16),
            pltpu.VMEM((chunk, buses), F32),
            pltpu.VMEM((lines, chunk), F32),
            pltpu.VMEM((planes, chunk, lines), F32),
            pltpu.VMEM((planes, bus_count - 1, chunk, lines), F32),
            pltpu.VMEM((2 * chunk, lines), BF16),
            pltpu.VMEM((chunk, lines), jnp.int32),
            pltpu.VMEM((4, hours, buses), F32),
            pltpu.VMEM((planes, 2, hours, buses), F32),
            pltpu.VMEM((planes, hours, buses), F32),
            pltpu.VMEM((planes, hours, buses), F32),
            pltpu.VMEM((hours, stores), F32),
            pltpu.VMEM((planes, 4, 8, stores), F32),
            dma((1,)),
            dma((2, planes)), dma((planes,)),
            dma((planes,)), dma((planes,)),
            dma((2, planes)), dma((2, planes)),
            dma((planes, bus_count - 1)), dma((planes, bus_count - 1)),
            dma((planes, 2, 2)), dma((planes, 2, 2)),
            dma((planes, 2)), dma((planes, 2)),
            dma((planes, 2)), dma((planes, 2)),
            dma((planes + 1,)), dma((planes + 1,)),
        ],
        compiler_params=pltpu.CompilerParams(
            collective_id=0, has_side_effects=True, vmem_limit_bytes=60 * 2**20
        ),
        cost_estimate=pl.CostEstimate(
            flops=12 * all_hours * lines * buses,
            bytes_accessed=4 * (lines * buses + all_hours * (buses + lines)),
            transcendentals=0,
        ),
    )(
        injections, shift_factors, line_rating, retention, discharge[None], profile,
        storage_bus[None], online_hour[None],
    )
    return (bus_adjoint, size_grad[0])


def solution(mesh):
    planes, bus_count = mesh.shape["line"] // 4, mesh.shape["bus"]
    in_specs = (
        P("line", "bus"),
        P("line", "bus"),
        P(None, "line"),
        P("line", "bus"),
        P("bus"),
        P("line", "bus"),
        P("bus"),
        P("bus"),
    )
    out_specs = (P("line", "bus"), P("bus"))
    return jax.shard_map(
        functools.partial(on_device, planes, bus_count),
        mesh=mesh, in_specs=in_specs, out_specs=out_specs, check_vma=False,
    )
```

```python
import functools
import math

import jax
import jax.numpy as jnp
from jax import lax
from jax.experimental import pallas as pl
from jax.experimental.pallas import tpu as pltpu
from jax.sharding import PartitionSpec as P

MESH = pl.DeviceIdType.MESH
F32, BF16 = jnp.float32, jnp.bfloat16


def split(value):
    high = value.astype(BF16)
    return high, (value - high.astype(F32)).astype(BF16)


def dot3(a_hi, a_lo, b_hi, b_lo, dims):
    dot = functools.partial(
        lax.dot_general, dimension_numbers=(dims, ((), ())), preferred_element_type=F32
    )
    return dot(a_hi, b_hi) + (dot(a_hi, b_lo) + dot(a_lo, b_hi))


def tile_of(width, most):
    return math.gcd(width, most)


def kernel(
    planes, bus_count,
    inj, factors, rating, retention, discharge, profile, storage_bus, online,
    out, size, gathered,
    s_hi, s_lo, stage, turned, flows, flows_in, a_hi, a_lo, limit, part,
    from_core, from_x, from_z, source, all_stats,
    local_sem,
    gz_send, gz_recv, gx_send, gx_recv, gc_send, gc_recv,
    y_send, y_recv, rc_send, rc_recv, rx_send, rx_recv, rz_send, rz_recv, st_send, st_recv,
):
    line, bus = lax.axis_index("line"), lax.axis_index("bus")
    z, x, c = line // 4, (line // 2) % 2, line % 2
    me = 2 * x + c
    hours, buses = inj.shape
    lines = factors.shape[0]
    chunk = 4 * hours

    def at(plane, column, core):
        return (plane * 4 + column * 2 + core, bus)

    sibling, across = at(z, x, 1 - c), at(z, 1 - x, c)

    def plane_of(s):
        above = planes - 1 - z
        up = jnp.where(s <= above, z + s, z - (s - above))
        down = jnp.where(s <= z, z - s, s)
        return jnp.where(z <= above, up, down)

    def rows(block):
        return pl.ds(pl.multiple_of(block * hours, hours), hours)

    def block_copy(plane, block, send, recv, target):
        ref = gathered.at[plane, rows(block)]
        return pltpu.make_async_remote_copy(
            src_ref=ref, dst_ref=ref, send_sem=send, recv_sem=recv,
            device_id=target, device_id_type=MESH,
        )

    def along_z(plane, way, target_plane):
        return block_copy(
            plane, me, gz_send.at[way, plane], gz_recv.at[plane], at(target_plane, x, c)
        )

    def to_across(plane):
        return block_copy(plane, me, gx_send.at[plane], gx_recv.at[plane], across)

    def from_across(plane):
        return block_copy(
            plane, 2 * (1 - x) + c, gx_send.at[plane], gx_recv.at[plane], across
        )

    def to_sibling(plane, k):
        block = 2 * (x if k == 0 else 1 - x) + c
        return block_copy(plane, block, gc_send.at[k, plane], gc_recv.at[k, plane], sibling)

    def from_sibling(plane, k):
        block = 2 * (x if k == 0 else 1 - x) + 1 - c
        return block_copy(plane, block, gc_send.at[k, plane], gc_recv.at[k, plane], sibling)

    def goes_up(plane):
        return (plane <= z) & (z + 1 < planes)

    def goes_down(plane):
        return (plane >= z) & (z > 0)

    def pass_on(plane):
        @pl.when(plane != z)
        def _():
            along_z(plane, 0, z).wait_recv()

        @pl.when(goes_up(plane))
        def _():
            along_z(plane, 0, z + 1).start()

        @pl.when(goes_down(plane))
        def _():
            along_z(plane, 1, z - 1).start()

        to_sibling(plane, 0).start()

    def pass_on_at(distance):
        @pl.when(z - distance >= 0)
        def _():
            pass_on(z - distance)

        @pl.when(z + distance < planes)
        def _():
            pass_on(z + distance)

    def forward_across(s):
        plane = plane_of(s)
        from_across(plane).wait_recv()
        to_sibling(plane, 1).start()

    def flow_copy(s, r):
        return pltpu.make_async_remote_copy(
            src_ref=flows.at[s], dst_ref=flows_in.at[s, r - 1],
            send_sem=y_send.at[s, r - 1], recv_sem=y_recv.at[s, r - 1],
            device_id=(line, (bus + r) % bus_count), device_id_type=MESH,
        )

    def first_product(s):
        plane = plane_of(s)
        from_sibling(plane, 0).wait_recv()
        from_sibling(plane, 1).wait_recv()
        load = pltpu.make_async_copy(gathered.at[plane], stage, local_sem.at[0])
        load.start()
        load.wait()
        width = tile_of(buses, 1024)
        turned[...] = jnp.zeros_like(turned)

        @pl.loop(0, buses // width)
        def _(n):
            here = pl.ds(pl.multiple_of(n * width, width), width)
            x_hi, x_lo = split(stage[:, here])
            turned[...] += dot3(s_hi[:, here], s_lo[:, here], x_hi, x_lo, ((1,), (1,)))

        step = tile_of(lines, 128)

        @pl.loop(0, lines // step)
        def _(n):
            here = pl.ds(pl.multiple_of(n * step, step), step)
            flows[s, :, here] = turned[here].T

        for r in range(1, bus_count):
            flow_copy(s, r).start()

    half = buses // 2

    def columns(h):
        return pl.ds(h * half, half)

    def core_copy(s, k, h):
        return pltpu.make_async_remote_copy(
            src_ref=part.at[2 * k + 1 - c, :, columns(h)],
            dst_ref=from_core.at[s, k, :, columns(h)],
            send_sem=rc_send.at[s, k, h], recv_sem=rc_recv.at[s, k, h],
            device_id=sibling, device_id_type=MESH,
        )

    def x_copy(s, h):
        return pltpu.make_async_remote_copy(
            src_ref=from_core.at[s, 1 - x, :, columns(h)],
            dst_ref=from_x.at[s, :, columns(h)],
            send_sem=rx_send.at[s, h], recv_sem=rx_recv.at[s, h],
            device_id=across, device_id_type=MESH,
        )

    def z_copy(s, h, target, slot):
        return pltpu.make_async_remote_copy(
            src_ref=from_x.at[s, :, columns(h)], dst_ref=from_z.at[slot, :, columns(h)],
            send_sem=rz_send.at[s, h], recv_sem=rz_recv.at[slot, h],
            device_id=at(target, x, c), device_id_type=MESH,
        )

    def second_product(s):
        plane = plane_of(s)
        here = pl.ds(pl.multiple_of(plane * chunk, chunk), chunk)
        load = pltpu.make_async_copy(rating.at[here], limit, local_sem.at[0])
        load.start()
        for r in range(1, bus_count):
            flow_copy(s, r).wait_recv()
        load.wait()
        step = tile_of(chunk, 32)

        @pl.loop(0, chunk // step)
        def _(i):
            here = pl.ds(pl.multiple_of(i * step, step), step)
            total = flows[s, here]
            for r in range(1, bus_count):
                total = total + flows_in[s, r - 1, here]
            bound = limit[here].astype(F32) * 0.01
            adjoint = jnp.where(
                total > bound, total - bound, jnp.where(total < -bound, total + bound, 0.0)
            )
            a_hi[here], a_lo[here] = split(adjoint)

    def second_half(s, h):
        width = tile_of(half, 512)

        @pl.loop(0, half // width)
        def _(n):
            here = pl.ds(pl.multiple_of(h * half + n * width, width), width)
            value = dot3(a_hi[...], a_lo[...], s_hi[:, here], s_lo[:, here], ((1,), (0,)))
            for block in range(4):
                part[block, :, here] = value[block * hours : (block + 1) * hours]

        for k in range(2):
            core_copy(s, k, h).start()

    def add_to(ref, other, h=None):
        step = tile_of(hours, 8)
        cols = pl.ds(0, buses) if h is None else columns(h)

        @pl.loop(0, hours // step)
        def _(i):
            here = pl.ds(pl.multiple_of(i * step, step), step)
            ref[here, cols] += other[here, cols]

    def reduce_across(s, h):
        for k in range(2):
            core_copy(s, k, h).wait_recv()
        add_to(from_core.at[s, 1 - x], part.at[2 * (1 - x) + c], h)
        x_copy(s, h).start()
        add_to(from_core.at[s, x], part.at[me], h)

    def reduce_along(s):
        for h in range(2):
            x_copy(s, h).wait_recv()
            add_to(from_x.at[s], from_core.at[s, x], h)

            @pl.when(s > 0)
            def _():
                z_copy(s, h, plane_of(s), z).start()

    def stat_copy(step, r=1):
        pair = 2 * x
        src, target = (
            (all_stats.at[z, pl.ds(me, 1)], sibling),
            (all_stats.at[z, pl.ds(pair, 2)], across),
            (all_stats.at[z], at((z + r) % planes, x, c)),
        )[step]
        return pltpu.make_async_remote_copy(
            src_ref=src, dst_ref=src,
            send_sem=st_send.at[step + r - 1], recv_sem=st_recv.at[step + r - 1],
            device_id=target, device_id_type=MESH,
        )

    def stat_arrival(step, r=1):
        plane = (z - r + planes) % planes
        ref = (
            all_stats.at[z, pl.ds(2 * x + 1 - c, 1)],
            all_stats.at[z, pl.ds(2 * (1 - x), 2)],
            all_stats.at[plane],
        )[step]
        return pltpu.make_async_remote_copy(
            src_ref=ref, dst_ref=ref,
            send_sem=st_send.at[step + r - 1], recv_sem=st_recv.at[step + r - 1],
            device_id=sibling, device_id_type=MESH,
        )

    barrier = pltpu.get_barrier_semaphore()
    mine = pltpu.make_async_copy(inj, gathered.at[z, rows(me)], local_sem.at[0])
    mine.start()
    for target in (sibling, across):
        pl.semaphore_signal(barrier, inc=1, device_id=target, device_id_type=MESH)
    for r in range(1, planes):
        pl.semaphore_signal(
            barrier, inc=1, device_id=at((z + r) % planes, x, c), device_id_type=MESH
        )
    for r in range(1, bus_count):
        pl.semaphore_signal(
            barrier, inc=1, device_id=(line, (bus + r) % bus_count), device_id_type=MESH
        )
    mine.wait()
    pl.semaphore_wait(barrier, planes + bus_count)
    pass_on(z)
    to_across(z).start()

    group = tile_of(lines, chunk)

    def factor_load(i):
        here = pl.ds(pl.multiple_of(i * group, group), group)
        return pltpu.make_async_copy(factors.at[here], stage.at[pl.ds(0, group)], local_sem.at[0])

    @pl.loop(0, lines // group)
    def _(i):
        factor_load(i).start()
        factor_load(i).wait()
        step = tile_of(group, 16)

        @pl.loop(0, group // step)
        def _(j):
            here = pl.ds(pl.multiple_of(j * step, step), step)
            there = pl.ds(pl.multiple_of(i * group + j * step, step), step)
            s_hi[there], s_lo[there] = split(stage[here])

    @pl.loop(0, planes + 4)
    def _(t):
        @pl.when(t + 1 < planes)
        def _():
            pass_on_at(t + 1)
            to_across(plane_of(t + 1)).start()

        @pl.when(t < planes)
        def _():
            forward_across(t)

        @pl.when((t >= 3) & (t < planes + 3))
        def _():
            s = (t - 2) % planes
            reduce_across(s, 0)
            reduce_across(s, 1)
            for h in range(2):
                for k in range(2):
                    core_copy(s, k, h).wait_send()

        @pl.when(t >= 4)
        def _():
            reduce_along((t - 3) % planes)

        @pl.when(t < planes)
        def _():
            first_product(t)

        @pl.when((t >= 2) & (t < planes + 2))
        def _():
            s = (t - 1) % planes
            second_product(s)
            second_half(s, 0)
            second_half(s, 1)

    total = from_x.at[0]
    for r in range(1, planes):
        other = (z + r) % planes
        for h in range(2):
            z_copy(0, h, other, other).wait_recv()
        add_to(total, from_z.at[other])
    store = pltpu.make_async_copy(total, out, local_sem.at[0])
    store.start()

    width = tile_of(buses, 512)
    source[...] = jnp.zeros_like(source)

    @pl.loop(0, buses // width)
    def _(n):
        here = pl.ds(pl.multiple_of(n * width, width), width)
        place = lax.broadcasted_iota(jnp.int32, (width, source.shape[1]), 0)
        chosen = jnp.where(place + (bus * buses + n * width) == storage_bus[...], 1.0, 0.0).astype(BF16)
        left = total[:, here]
        for _ in range(3):
            high = left.astype(BF16)
            left = left - high.astype(F32)
            source[...] += jnp.dot(high, chosen, preferred_element_type=F32)

    def hour_back(i, carried):
        carry, gain, fixed, slope = carried
        t = hours - 1 - i
        keep = retention[pl.ds(t, 1), :]
        weight = jnp.where(line * hours + t >= online[...], profile[pl.ds(t, 1), :], 0.0)
        costate = discharge[...] * source[pl.ds(t, 1), :] + carry
        return (keep * costate, keep * gain, fixed + costate * weight, slope + gain * weight)

    all_stats[z, me] = jnp.zeros(all_stats.shape[2:], F32)
    zero = jnp.zeros((1, source.shape[1]), F32)
    done = lax.fori_loop(0, hours, hour_back, (zero, zero + 1.0, zero, zero))
    for i in range(4):
        all_stats[z, me, i : i + 1, :] = done[i]
    for step in range(2):
        stat_copy(step).start()
        stat_arrival(step).wait_recv()
    for r in range(1, planes):
        stat_copy(2, r).start()
    for r in range(1, planes):
        stat_arrival(2, r).wait_recv()

    def block_back(i, carried):
        carry, total = carried
        block = 4 * planes - 1 - i
        offset, gain, fixed, slope = (
            all_stats[block // 4, block % 4, row : row + 1, :] for row in range(4)
        )
        return (offset + gain * carry, total + (fixed + slope * carry))

    sums = lax.fori_loop(0, 4 * planes, block_back, (zero, zero))
    size[...] = sums[1] / math.sqrt(4 * planes * hours)
    for step in range(2):
        stat_copy(step).wait_send()
    for r in range(1, planes):
        stat_copy(2, r).wait_send()
    store.wait()

    @pl.loop(0, planes)
    def _(s):
        plane = plane_of(s)

        @pl.when(goes_up(plane))
        def _():
            along_z(plane, 0, z + 1).wait_send()

        @pl.when(goes_down(plane))
        def _():
            along_z(plane, 1, z - 1).wait_send()

        to_across(plane).wait_send()
        for k in range(2):
            to_sibling(plane, k).wait_send()
        for r in range(1, bus_count):
            flow_copy(s, r).wait_send()
        for h in range(2):
            x_copy(s, h).wait_send()

        @pl.when(s > 0)
        def _():
            for h in range(2):
                z_copy(s, h, plane_of(s), z).wait_send()


def on_device(
    planes, bus_count,
    injections, shift_factors, line_rating, retention, discharge, profile, storage_bus, online_hour,
):
    hours, buses = injections.shape
    lines = shift_factors.shape[0]
    stores = retention.shape[1]
    chunk = 4 * hours
    all_hours = chunk * planes
    hbm, vmem = pl.BlockSpec(memory_space=pl.ANY), pl.BlockSpec(memory_space=pltpu.VMEM)
    dma = pltpu.SemaphoreType.DMA
    bus_adjoint, size_grad, _ = pl.pallas_call(
        functools.partial(kernel, planes, bus_count),
        out_shape=(
            jax.ShapeDtypeStruct((hours, buses), F32),
            jax.ShapeDtypeStruct((1, stores), F32),
            jax.ShapeDtypeStruct((planes, chunk, buses), F32),
        ),
        in_specs=[hbm, hbm, hbm, vmem, vmem, vmem, vmem, vmem],
        out_specs=(hbm, vmem, hbm),
        scratch_shapes=[
            pltpu.VMEM((lines, buses), BF16),
            pltpu.VMEM((lines, buses), BF16),
            pltpu.VMEM((chunk, buses), F32),
            pltpu.VMEM((lines, chunk), F32),
            pltpu.VMEM((planes, chunk, lines), F32),
            pltpu.VMEM((planes, bus_count - 1, chunk, lines), F32),
            pltpu.VMEM((chunk, lines), BF16),
            pltpu.VMEM((chunk, lines), BF16),
            pltpu.VMEM((chunk, lines), jnp.int32),
            pltpu.VMEM((4, hours, buses), F32),
            pltpu.VMEM((planes, 2, hours, buses), F32),
            pltpu.VMEM((planes, hours, buses), F32),
            pltpu.VMEM((planes, hours, buses), F32),
            pltpu.VMEM((hours, stores), F32),
            pltpu.VMEM((planes, 4, 8, stores), F32),
            dma((1,)),
            dma((2, planes)), dma((planes,)),
            dma((planes,)), dma((planes,)),
            dma((2, planes)), dma((2, planes)),
            dma((planes, bus_count - 1)), dma((planes, bus_count - 1)),
            dma((planes, 2, 2)), dma((planes, 2, 2)),
            dma((planes, 2)), dma((planes, 2)),
            dma((planes, 2)), dma((planes, 2)),
            dma((planes + 1,)), dma((planes + 1,)),
        ],
        compiler_params=pltpu.CompilerParams(
            collective_id=0, has_side_effects=True, vmem_limit_bytes=60 * 2**20
        ),
        cost_estimate=pl.CostEstimate(
            flops=12 * all_hours * lines * buses,
            bytes_accessed=4 * (lines * buses + all_hours * (buses + lines)),
            transcendentals=0,
        ),
    )(
        injections, shift_factors, line_rating, retention, discharge[None], profile,
        storage_bus[None], online_hour[None],
    )
    return (bus_adjoint, size_grad[0])


def solution(mesh):
    planes, bus_count = mesh.shape["line"] // 4, mesh.shape["bus"]
    in_specs = (
        P("line", "bus"),
        P("line", "bus"),
        P(None, "line"),
        P("line", "bus"),
        P("bus"),
        P("line", "bus"),
        P("bus"),
        P("bus"),
    )
    out_specs = (P("line", "bus"), P("bus"))
    return jax.shard_map(
        functools.partial(on_device, planes, bus_count),
        mesh=mesh, in_specs=in_specs, out_specs=out_specs, check_vma=False,
    )
```
